128 devices in a mesh: snap: 4 (over z), tile: 16 (over x, y), level: 2 (over core).
Axes of the slice: x: 4, y: 4, z: 4, core: 2. Of those that a mesh axis runs over, the one named last changes fastest.
Arguments:
- coarse: bfloat16 [4, 262144, 512], P(None, ('tile', 'level'), 'snap'), may hold values from -100 to 100
- fine_cells: bfloat16 [768, 4, 512, 512], P(('tile', 'level'), None, None, 'snap'), may hold values from -6 to 6
- patch_block: int32 [768], replicated, may hold values from 0 to 4095, as said below
- fine_map: int32 [512], replicated, may hold values from 0 to 63, as said below
- field_weight: float32 [4], replicated, may hold values from 0.25 to 4
Outputs:
- gram_matrix: float32 [512, 512], P(('snap', 'tile', 'level'))
- restricted: bfloat16 [4, 2048, 64, 512], P(None, ('tile', 'level'), None, 'snap')
The draws below stay inside these ranges and needn't reach their ends.
Inputs may be any that keep to these rules, and one draw needn't show every extreme that they name: `patch_block`: all entries are distinct. At most 2 patches of one owner lie in the boxes of one tile owner, and some owner and tile owner reach 2. `fine_map`: each value appears exactly 8 times.
All inputs are finite; a program needn't handle non-finite values.
Results may differ from the reference program's by a relative error of at most 0.001.
Values may be sent and summed in bfloat16 or wider, within the bound.
No kernel may reach another device: no remote copies, remote signals or barrier semaphores. Data moves between devices by JAX's collectives and lax.ppermute only.
A program may use at most 192 MiB of HBM per device.

```python
import math
import jax
import jax.numpy as jnp
from jax import lax

S = 512
F = 4
CD = 2048
PB = 64
FINE = 512
PATCH_DEV = 24
SLOTS = 64
CELLS = 262144
PATCHES = 768
N_SNAP = 4
N_TILE = 16
N_LEVEL = 2


def shuffled_patches(subkey):
    return jax.random.permutation(subkey, PATCH_DEV)


def shuffled_slots(subkey):
    return jax.random.permutation(subkey, SLOTS)


def draw_patch_block(key, part):
    key = jax.random.fold_in(key, 7)
    subkeys = jax.random.split(key, 5)
    owners = N_TILE * N_LEVEL
    capacity = SLOTS // owners
    blocks_dev = CD * N_SNAP // PB
    stride = blocks_dev // SLOTS
    hot_count = max(1, owners // 8)
    hot_owner = jax.random.permutation(subkeys[0], owners)[:hot_count]
    slot_ids = jnp.arange(SLOTS, dtype=jnp.int32)
    slot_owner = slot_ids // capacity
    is_hot = jnp.any(slot_owner[:, None] == hot_owner[None, :], axis=1).astype(jnp.int32)
    tie_break = jax.random.randint(subkeys[1], (owners, SLOTS), 0, 4096)
    scores = (tie_break + 4096 * is_hot[None, :]) * SLOTS + slot_ids[None, :]
    unused, chosen = lax.top_k(scores, PATCH_DEV)
    shuffle = jax.vmap(shuffled_patches)(jax.random.split(subkeys[2], owners))
    chosen = jnp.take_along_axis(chosen, shuffle, axis=1)
    dest_owner = chosen // capacity
    occurrence = chosen % capacity
    arrival = jax.vmap(shuffled_slots)(jax.random.split(subkeys[3], owners))
    incoming = jnp.arange(owners, dtype=jnp.int32)[:, None] * capacity + occurrence
    placed = arrival[dest_owner, incoming]
    jitter = jax.random.randint(subkeys[4], (owners, PATCH_DEV), 0, stride)
    drawn = dest_owner * blocks_dev + placed * stride + jitter
    return drawn.reshape(owners * PATCH_DEV).astype(jnp.int32)


def draw_fine_map(key, part):
    key = jax.random.fold_in(key, 3)
    return (jax.random.permutation(key, FINE) // 8).astype(jnp.int32)


def draw_coarse(key, part):
    key = jax.random.fold_in(key, 5)
    subkeys = jax.random.split(key, 5)
    cells = CD * N_SNAP * N_TILE * N_LEVEL
    block_count = cells // CD
    fluctuation = jnp.clip(jax.random.normal(subkeys[0], (F, cells, S), jnp.float32), -6.0, 6.0)
    region = jnp.ones((1, cells, 1), jnp.float32)
    spatial_mode = jnp.clip(jax.random.normal(subkeys[1], (F, cells, 1), jnp.float32), -6.0, 6.0)
    amplitude = jax.random.uniform(subkeys[2], (1, 1, S), jnp.float32, -1.0, 1.0)
    snap_scale = jax.random.uniform(subkeys[3], (1, 1, S), jnp.float32, 0.5, 2.0)
    offset_block = jax.random.randint(subkeys[4], (), 0, block_count)
    paired = (jnp.arange(S, dtype=jnp.int32) * 5 + offset_block) % block_count
    in_pair = (jnp.arange(cells, dtype=jnp.int32) // CD)[None, :, None] == paired[None, None, :]
    drawn = snap_scale * region * (fluctuation + 0.8 * amplitude * spatial_mode)
    drawn = drawn * jnp.where(in_pair, 3.0, 1.0)
    return drawn.astype(jnp.bfloat16)


def steps_of(own_key, shape, cuts, smallest, largest):
    loudness = 1.0
    for axis_at, shards_of in cuts:
        steps = jax.random.uniform(jax.random.fold_in(jax.random.fold_in(own_key, 6), axis_at), (shards_of,), jnp.float32, smallest / len(cuts), largest / len(cuts))
        loudness = loudness * jnp.repeat(jnp.exp(steps), shape[axis_at] // shards_of).reshape((-1,) + (1,) * (len(shape) - 1 - axis_at))
    return loudness


def noise(stream_key, shape, scale, limit, shards=(), kind=jnp.bfloat16):
    values = jax.random.normal(stream_key, shape, jnp.float32) * scale
    if len(shards) > 0:
        values = steps_of(stream_key, shape, shards, -0.22, 0.18) * values
    return jnp.clip(values, min=-limit, max=limit).astype(kind)


def setup_inputs(seed: int = 0) -> dict:
    arg_keys = jax.random.split(jax.random.key(seed), 6)
    coarse = draw_coarse(jax.random.fold_in(arg_keys[5], 71), 0)
    fine_cells = noise(arg_keys[1], (PATCHES, F, FINE, S), 1.0, 6.0, ((0, 32), (3, 4)))
    patch_block = draw_patch_block(jax.random.fold_in(arg_keys[5], 71), 0)
    fine_map = draw_fine_map(jax.random.fold_in(arg_keys[5], 71), 0)
    field_weight = jnp.clip(jnp.exp(jax.random.uniform(arg_keys[4], (F,), jnp.float32, math.log(0.25), math.log(4.0))), 0.25, 4.0)
    return {"coarse": coarse, "fine_cells": fine_cells, "patch_block": patch_block, "fine_map": fine_map, "field_weight": field_weight}


def reference(coarse, fine_cells, patch_block, fine_map, field_weight):
    owners = N_TILE * N_LEVEL
    capacity = SLOTS // owners
    blocks_dev = CELLS // PB // owners
    patch_count = patch_block.shape[0]
    target = patch_block // blocks_dev
    owner_grid = target.reshape(owners, PATCH_DEV)
    position = jnp.arange(PATCH_DEV, dtype=jnp.int32)
    earlier = position[None, :] < position[:, None]
    same_target = owner_grid[:, :, None] == owner_grid[:, None, :]
    rank_same = jnp.sum((same_target & earlier[None]).astype(jnp.int32), axis=2).reshape(patch_count)
    source = jnp.arange(patch_count, dtype=jnp.int32) // PATCH_DEV
    out_row = (target * SLOTS + source * capacity + rank_same).astype(jnp.int32)
    averaging = (fine_map[:, None] == jnp.arange(PB, dtype=jnp.int32)[None, :]).astype(jnp.float32) * 0.125

    def restrict_bundle(bundle):
        widened = bundle.astype(jnp.float32)
        return jnp.einsum("pfes,eb->fpbs", widened, averaging, precision=lax.Precision.HIGHEST).astype(jnp.bfloat16)

    grouped = lax.map(restrict_bundle, fine_cells.reshape(owners, PATCH_DEV, F, FINE, S))
    restricted_patch = jnp.moveaxis(grouped, 1, 0).reshape(F, patch_count, PB, S)
    restricted = jnp.zeros((F, owners * SLOTS, PB, S), jnp.bfloat16).at[:, out_row].set(restricted_patch)
    composite = coarse.reshape(F, CELLS // PB, PB, S).at[:, patch_block].set(restricted_patch)
    composite = composite.reshape(F, CELLS, S)
    devices = N_SNAP * owners

    def accumulate(index, running):
        cell_slab = lax.dynamic_slice_in_dim(composite, (index * CD).astype(jnp.int32), CD, 1)
        widened = cell_slab.astype(jnp.float32)
        per_field = jnp.einsum("fcs,fct->fst", widened, widened, precision=lax.Precision.HIGHEST)
        return running + jnp.sum(field_weight[:, None, None] * per_field, axis=0)

    gram_matrix = lax.fori_loop(0, devices, accumulate, jnp.zeros((S, S), jnp.float32))
    return gram_matrix / (F * CELLS), restricted
```

```python
import jax
import jax.numpy as jnp
from jax import lax
from jax.experimental import pallas as pl
from jax.experimental.pallas import tpu as pltpu
from jax.sharding import PartitionSpec as P

F = 4
PB = 64
SLOTS = 64
NZ = 4
OWNERS = 32
LANES = 128
QUARTER = SLOTS // NZ
GROUPS = ((0, 3), (3, 1))
S = NZ * LANES
SEND_ORDER = (1, 3, 2, 0)
XY = ("tile", "level")
ALL = ("snap", "tile", "level")
BF16, F32, I32 = jnp.bfloat16, jnp.float32, jnp.int32
ANY = pl.BlockSpec(memory_space=pl.ANY)
SMEM = pl.BlockSpec(memory_space=pltpu.SMEM)
VMEM = pl.BlockSpec(memory_space=pltpu.VMEM)
PARAMS = pltpu.CompilerParams(vmem_limit_bytes=58 * 2**20)


def cost(bytes_accessed, flops=0):
    return pl.CostEstimate(flops=flops, bytes_accessed=bytes_accessed, transcendentals=0)


def tables(patch_block, own, z, per_owner, blocks_dev):
    k = jnp.arange(SLOTS, dtype=I32)
    order = QUARTER * ((z + k // QUARTER) % NZ) + k % QUARTER
    boxes = jnp.arange(blocks_dev, dtype=I32)
    local = patch_block - own * blocks_dev
    free = jnp.all(local[None, :] != boxes[:, None], axis=1)
    rank_free = jnp.sum((free[None, :] & (boxes[None, :] < boxes[:, None])).astype(I32), axis=1)
    place = jnp.where(free, rank_free, -1)
    first = jnp.sum(jnp.where(place[None, :] == order[:, None], boxes[None, :], 0), axis=1)

    target = patch_block // blocks_dev
    own_target = lax.dynamic_slice_in_dim(target, own * per_owner, per_owner)
    p = jnp.arange(per_owner, dtype=I32)
    same = (own_target[None, :] == own_target[:, None]) & (p[None, :] < p[:, None])
    slot = own_target * (SLOTS // OWNERS) + jnp.sum(same.astype(I32), axis=1)
    has_patch = jnp.any(slot[None, :] == k[:, None], axis=1).astype(I32)

    arrived = jnp.sum((target.reshape(OWNERS, per_owner) == own).astype(I32), axis=1)
    filled = (arrived[:, None] > jnp.arange(SLOTS // OWNERS, dtype=I32)[None, :]).reshape(SLOTS)
    empty_before = jnp.sum(((~filled)[None, :] & (k[None, :] < order[:, None])).astype(I32), axis=1)
    second = jnp.sum(jnp.where(place[None, :] == SLOTS + empty_before[:, None], boxes[None, :], 0), axis=1)
    filled_at = jnp.any(filled[None, :] & (k[None, :] == order[:, None]), axis=1)
    pick = jnp.where(filled_at, -1, second)
    return first, slot, has_patch, order, pick


def stage_out(stage, outs, into, away):
    for n, out in enumerate(outs):
        pltpu.make_async_copy(out, stage.at[n], into.at[n]).wait()
        pltpu.make_async_copy(stage.at[n], out, away.at[n]).start()
    for n, out in enumerate(outs):
        pltpu.make_async_copy(stage.at[n], out, away.at[n]).wait()


def gather_kernel(parts, first_ref, coarse_ref, *rest):
    outs, (stage, into, away) = rest[:-3], rest[-3:]
    for n, r in enumerate(parts):
        for j in range(QUARTER):
            pltpu.make_async_copy(coarse_ref.at[:, first_ref[r * QUARTER + j]], stage.at[n, j], into.at[n]).start()
    stage_out(stage, outs, into, away)


def gather_free(first, coarse, parts):
    shape = (QUARTER, F, PB, LANES)
    return pl.pallas_call(
        lambda *refs: gather_kernel(parts, *refs),
        out_shape=[jax.ShapeDtypeStruct(shape, BF16) for _ in parts],
        in_specs=[SMEM, ANY],
        out_specs=[ANY for _ in parts],
        scratch_shapes=[pltpu.VMEM((len(parts), *shape), BF16)] + [pltpu.SemaphoreType.DMA((NZ,))] * 2,
        compiler_params=PARAMS,
        cost_estimate=cost(2 * len(parts) * QUARTER * F * PB * LANES * 2),
    )(first, coarse)


def restrict_kernel(steps, group, fields, slot_ref, has_ref, map_ref, fine_ref, after_ref, out_ref, averaging, zeros, results, sem):
    step = pl.program_id(0)

    @pl.when(step == 0)
    def _():
        e_of = map_ref[...]
        b = lax.broadcasted_iota(I32, averaging.shape, 0)
        averaging[...] = jnp.where(e_of == b, 0.125, 0.0).astype(BF16)
        zeros[...] = jnp.zeros_like(zeros)
        for q in range(SLOTS):

            @pl.when(has_ref[q] == 0)
            def _(q=q):
                pltpu.make_async_copy(zeros, out_ref.at[q], sem).start()

    for i in range(group):
        p = step * group + i
        wide = jnp.concatenate([fine_ref[i, f] for f in range(fields)], axis=1)
        mean = jnp.dot(averaging[...], wide, preferred_element_type=F32).astype(BF16)
        for f in range(fields):
            results[p, f] = mean[:, f * LANES : (f + 1) * LANES]
        pltpu.make_async_copy(results.at[p], out_ref.at[slot_ref[p]], sem).start()

    @pl.when(step == steps - 1)
    def _():
        pltpu.make_async_copy(out_ref, out_ref, sem).wait()


def restrict(slot, has_patch, fine_map, fine_cells, at, fields, after):
    per_owner, fine = fine_cells.shape[0], fine_cells.shape[2]
    group = 4
    steps = per_owner // group
    return pl.pallas_call(
        lambda *refs: restrict_kernel(steps, group, fields, *refs),
        grid=(steps,),
        out_shape=jax.ShapeDtypeStruct((SLOTS, fields, PB, LANES), BF16),
        in_specs=[
            SMEM,
            SMEM,
            pl.BlockSpec((1, fine), lambda i: (0, 0)),
            pl.BlockSpec((group, fields, fine, LANES), lambda i: (i, at // fields, 0, 0)),
            ANY,
        ],
        out_specs=ANY,
        scratch_shapes=[
            pltpu.VMEM((PB, fine), BF16),
            pltpu.VMEM((fields, PB, LANES), BF16),
            pltpu.VMEM((per_owner, fields, PB, LANES), BF16),
            pltpu.SemaphoreType.DMA,
        ],
        compiler_params=PARAMS,
        cost_estimate=cost(fields * 2**22, 2 * per_owner * fields * PB * fine * LANES),
    )(slot, has_patch, fine_map.reshape(1, fine), fine_cells, after)


def merge_kernel(at, count, order_ref, pick_ref, received_ref, coarse_ref, *rest):
    outs, (stage, into, away) = rest[:-3], rest[-3:]
    fields = pl.ds(at, count)
    for n, r in enumerate(SEND_ORDER):
        for j in range(QUARTER):
            k = r * QUARTER + j
            box = pick_ref[k]

            @pl.when(box < 0)
            def _(n=n, j=j, k=k):
                pltpu.make_async_copy(received_ref.at[order_ref[k]], stage.at[n, j], into.at[n]).start()

            @pl.when(box >= 0)
            def _(n=n, j=j, box=box):
                pltpu.make_async_copy(coarse_ref.at[fields, box], stage.at[n, j], into.at[n]).start()

    stage_out(stage, [outs[r] for r in SEND_ORDER], into, away)


def merge(order, pick, received, coarse, at):
    count = received.shape[1]
    shape = (QUARTER, count, PB, LANES)
    return pl.pallas_call(
        lambda *refs: merge_kernel(at, count, *refs),
        out_shape=[jax.ShapeDtypeStruct(shape, BF16)] * NZ,
        in_specs=[SMEM, SMEM, ANY, ANY],
        out_specs=[ANY] * NZ,
        scratch_shapes=[pltpu.VMEM((NZ, *shape), BF16)] + [pltpu.SemaphoreType.DMA((NZ,))] * 2,
        compiler_params=PARAMS,
        cost_estimate=cost(count * 2**21),
    )(order, pick, received, coarse)


def output_kernel(low_ref, high_ref, out_ref, stage, into, away):
    ins, outs = [], []
    for ref, (at, count) in zip((low_ref, high_ref), GROUPS):
        for i in range(count):
            f = at + i
            ins.append(pltpu.make_async_copy(ref.at[:, i], stage.at[f], into.at[f]))
            outs.append(pltpu.make_async_copy(stage.at[f], out_ref.at[f], away.at[f]))
    for copy in ins:
        copy.start()
    for copy, out in zip(ins, outs):
        copy.wait()
        out.start()
    for out in outs:
        out.wait()


def slot_output(low, high):
    return pl.pallas_call(
        output_kernel,
        out_shape=jax.ShapeDtypeStruct((F, SLOTS, PB, LANES), BF16),
        in_specs=[ANY, ANY],
        out_specs=ANY,
        scratch_shapes=[pltpu.VMEM((F, SLOTS, PB, LANES), BF16)] + [pltpu.SemaphoreType.DMA((F,))] * 2,
        compiler_params=PARAMS,
        cost_estimate=cost(8 * 2**20),
    )(low, high)


def gram_kernel(offset, weight_ref, x0, x1, x2, x3, before_ref, out_ref):
    f = pl.program_id(0)

    @pl.when(f == 0)
    def _():
        out_ref[...] = before_ref[...]

    cells = QUARTER * PB
    wide = jnp.concatenate([x[...].reshape(cells, LANES) for x in (x0, x1, x2, x3)], axis=1)
    product = lax.dot_general(wide, wide, (((0,), (0,)), ((), ())), preferred_element_type=F32)
    for b in range(NZ):
        out_ref[b] += weight_ref[offset + f] * product[:, b * LANES : (b + 1) * LANES]


def first_gram_kernel(weight_ref, x0, x1, x2, x3, out_ref):
    f = pl.program_id(0)

    @pl.when(f == 0)
    def _():
        out_ref[...] = jnp.zeros_like(out_ref)

    cells = QUARTER * PB
    wide = jnp.concatenate([x[...].reshape(cells, LANES) for x in (x0, x1, x2, x3)], axis=1)
    product = lax.dot_general(wide, wide, (((0,), (0,)), ((), ())), preferred_element_type=F32)
    for b in range(NZ):
        out_ref[b] += weight_ref[f] * product[:, b * LANES : (b + 1) * LANES]


def gram(weight, xs, before=None, offset=0):
    fields = xs[0].shape[1]
    block = pl.BlockSpec((QUARTER, 1, PB, LANES), lambda f: (0, f, 0, 0))
    whole = pl.BlockSpec((NZ, S, LANES), lambda f: (0, 0, 0))
    if before is None:
        kernel, more, extra = first_gram_kernel, (), []
    else:
        kernel, more, extra = (lambda *refs: gram_kernel(offset, *refs)), (before,), [whole]
    return pl.pallas_call(
        kernel,
        grid=(fields,),
        out_shape=jax.ShapeDtypeStruct((NZ, S, LANES), F32),
        in_specs=[SMEM] + [block] * NZ + extra,
        out_specs=whole,
        compiler_params=PARAMS,
        cost_estimate=cost(fields * 2**20 + 2**21, 2 * fields * QUARTER * PB * S * S),
    )(weight, *xs, *more)


def pieces_kernel(scale, z_ref, in_ref, out_ref):
    z = z_ref[0]
    rows = S // 128
    for a in range(NZ):
        ga = (a + z) % NZ
        for b in range(NZ):
            gb = (b + z) % NZ
            for i in range(rows):
                part = in_ref[b, pl.ds(a * LANES + i, LANES // rows, stride=rows), :]
                start = ga * (LANES // rows) * 16 + gb * rows + i
                out_ref[pl.ds(start, LANES // rows, stride=16), :] = part * scale


def pieces(z, total, scale):
    return pl.pallas_call(
        lambda *refs: pieces_kernel(scale, *refs),
        out_shape=jax.ShapeDtypeStruct((S * NZ, LANES), F32),
        in_specs=[SMEM, VMEM],
        out_specs=VMEM,
        compiler_params=PARAMS,
        cost_estimate=cost(2 * 2**20),
    )(z.reshape(1), total)


def shift(x, by):
    return lax.ppermute(x, "snap", [(i, (i + by) % NZ) for i in range(NZ)])


def exchange(sends):
    from_below = shift(sends[1], 1)
    from_above = shift(sends[3], 3)
    from_across = shift(sends[2], 2)
    return (sends[0], from_above, from_across, from_below)


def on_device(coarse, fine_cells, patch_block, fine_map, field_weight):
    own = lax.axis_index(XY).astype(I32)
    z = lax.axis_index("snap").astype(I32)
    per_owner = fine_cells.shape[0]
    blocks_dev = coarse.shape[1] // PB
    coarse_boxes = coarse.reshape(F, blocks_dev, PB, LANES)
    first, slot, has_patch, order, pick = tables(patch_block, own, z, per_owner, blocks_dev)

    up, down = gather_free(first, coarse_boxes, (1, 3))
    across, stay = gather_free(first, coarse_boxes, (2, 0))
    group_a = exchange((stay, up, across, down))

    received = []
    for (at, fields), after in zip(GROUPS, (up, across)):
        outgoing = restrict(slot, has_patch, fine_map, fine_cells, at, fields, after)
        if at:
            outgoing, received[0], group_a = lax.optimization_barrier((outgoing, received[0], group_a))
        received.append(lax.all_to_all(outgoing, XY, split_axis=0, concat_axis=0, tiled=True))
    restricted = slot_output(received[0], received[1])

    total = gram(field_weight, group_a)
    for (at, _), arrived in zip(GROUPS, received):
        group = exchange(merge(order, pick, arrived, coarse_boxes, at))
        total = gram(field_weight, group, total, at)

    cells_all = coarse.shape[1] * OWNERS
    shares = pieces(z, total, 1.0 / (F * cells_all))
    collected = lax.all_to_all(shares, ALL, split_axis=0, concat_axis=0, tiled=True)
    summed = jnp.sum(collected.reshape(128, NZ, NZ, LANES), axis=0)
    gram_matrix = summed.transpose(1, 0, 2).reshape(S // 128, S)
    return (gram_matrix, restricted)


def solution(mesh):
    return jax.shard_map(
        on_device,
        mesh=mesh,
        in_specs=(
            P(None, ("tile", "level"), "snap"),
            P(("tile", "level"), None, None, "snap"),
            P(),
            P(),
            P(),
        ),
        out_specs=(P(("snap", "tile", "level"), None), P(None, ("tile", "level"), None, "snap")),
        check_vma=False,
    )
```

```python
import jax
import jax.numpy as jnp
from jax import lax
from jax.experimental import pallas as pl
from jax.experimental.pallas import tpu as pltpu
from jax.sharding import PartitionSpec as P

F = 4
PB = 64
SLOTS = 64
NZ = 4
OWNERS = 32
LANES = 128
QUARTER = SLOTS // NZ
EARLY = 2
S = NZ * LANES
SEND_ORDER = (2, 1, 3, 0)
GRAM_ORDER = (0, 2, 1, 3)
XY = ("tile", "level")
ALL = ("snap", "tile", "level")
BF16, F32, I32 = jnp.bfloat16, jnp.float32, jnp.int32
ANY = pl.BlockSpec(memory_space=pl.ANY)
SMEM = pl.BlockSpec(memory_space=pltpu.SMEM)
VMEM = pl.BlockSpec(memory_space=pltpu.VMEM)
PARAMS = pltpu.CompilerParams(vmem_limit_bytes=58 * 2**20)


def cost(bytes_accessed, flops=0):
    return pl.CostEstimate(flops=flops, bytes_accessed=bytes_accessed, transcendentals=0)


def tables(patch_block, own, z, per_owner, blocks_dev):
    k = jnp.arange(SLOTS, dtype=I32)
    order = QUARTER * ((z + k // QUARTER) % NZ) + k % QUARTER
    boxes = jnp.arange(blocks_dev, dtype=I32)
    local = patch_block - own * blocks_dev
    free = jnp.all(local[None, :] != boxes[:, None], axis=1)
    rank_free = jnp.sum((free[None, :] & (boxes[None, :] < boxes[:, None])).astype(I32), axis=1)
    place = jnp.where(free, rank_free, -1)
    first = jnp.sum(jnp.where(place[None, :] == order[:, None], boxes[None, :], 0), axis=1)

    target = lax.shift_right_logical(patch_block, jnp.int32(blocks_dev.bit_length() - 1))
    own_target = lax.dynamic_slice_in_dim(target, own * per_owner, per_owner)
    p = jnp.arange(per_owner, dtype=I32)
    same = (own_target[None, :] == own_target[:, None]) & (p[None, :] < p[:, None])
    slot = own_target * (SLOTS // OWNERS) + jnp.sum(same.astype(I32), axis=1)
    has_patch = jnp.any(slot[None, :] == k[:, None], axis=1).astype(I32)

    arrived = jnp.sum((target.reshape(OWNERS, per_owner) == own).astype(I32), axis=1)
    filled = (arrived[:, None] > jnp.arange(SLOTS // OWNERS, dtype=I32)[None, :]).reshape(SLOTS)
    empty_before = jnp.sum(((~filled)[None, :] & (k[None, :] < order[:, None])).astype(I32), axis=1)
    second = jnp.sum(jnp.where(place[None, :] == SLOTS + empty_before[:, None], boxes[None, :], 0), axis=1)
    filled_at = jnp.any(filled[None, :] & (k[None, :] == order[:, None]), axis=1)
    pick = jnp.where(filled_at, -1, second)
    late = jnp.sum(jnp.where(place[None, :] == SLOTS + order[:, None], boxes[None, :] + 1, 0), axis=1) - 1
    return first, slot, has_patch, order, pick, late


def stage_out(stage, outs, into, away):
    for n, out in enumerate(outs):
        pltpu.make_async_copy(out, stage.at[n], into.at[n]).wait()
        pltpu.make_async_copy(stage.at[n], out, away.at[n]).start()
    for n, out in enumerate(outs):
        pltpu.make_async_copy(stage.at[n], out, away.at[n]).wait()


def gather_kernel(parts, first_ref, coarse_ref, after_ref, *rest):
    outs, (stage, into, away) = rest[:-3], rest[-3:]
    for n, r in enumerate(parts):
        for j in range(QUARTER):
            pltpu.make_async_copy(coarse_ref.at[:, first_ref[r * QUARTER + j]], stage.at[n, j], into.at[n]).start()
    stage_out(stage, outs, into, away)


def gather_free(first, coarse, parts, after):
    shape = (QUARTER, F, PB, LANES)
    return pl.pallas_call(
        lambda *refs: gather_kernel(parts, *refs),
        out_shape=[jax.ShapeDtypeStruct(shape, BF16) for _ in parts],
        in_specs=[SMEM, ANY, ANY],
        out_specs=[ANY for _ in parts],
        scratch_shapes=[pltpu.VMEM((len(parts), *shape), BF16)] + [pltpu.SemaphoreType.DMA((NZ,))] * 2,
        compiler_params=PARAMS,
        cost_estimate=cost(2 * len(parts) * QUARTER * F * PB * LANES * 2),
    )(first, coarse, after)


def restrict_kernel(steps, group, fields, slot_ref, has_ref, map_ref, fine_ref, after_ref, out_ref, plain_ref, averaging, zeros, results, sem, plain_sem):
    step = pl.program_id(0)

    @pl.when(step == 0)
    def _():
        e_of = map_ref[...]
        b = lax.broadcasted_iota(I32, averaging.shape, 0)
        averaging[...] = jnp.where(e_of == b, 0.125, 0.0).astype(BF16)
        zeros[...] = jnp.zeros_like(zeros)
        for q in range(SLOTS):

            @pl.when(has_ref[q] == 0)
            def _(q=q):
                pltpu.make_async_copy(zeros, out_ref.at[q], sem).start()

    for i in range(group):
        p = step * group + i
        wide = jnp.concatenate([fine_ref[i, f] for f in range(fields)], axis=1)
        mean = jnp.dot(averaging[...], wide, preferred_element_type=F32).astype(BF16)
        for f in range(fields):
            results[p, f] = mean[:, f * LANES : (f + 1) * LANES]
        pltpu.make_async_copy(results.at[p], out_ref.at[slot_ref[p]], sem).start()

    @pl.when(step == steps - 1)
    def _():
        plain = pltpu.make_async_copy(results.at[:, pl.ds(EARLY, fields - EARLY)], plain_ref, plain_sem)
        plain.start()
        plain.wait()
        pltpu.make_async_copy(out_ref, out_ref, sem).wait()


def restrict(slot, has_patch, fine_map, fine_cells, after):
    per_owner, fields, fine, _ = fine_cells.shape
    group = 4
    steps = per_owner // group
    return pl.pallas_call(
        lambda *refs: restrict_kernel(steps, group, fields, *refs),
        grid=(steps,),
        out_shape=[
            jax.ShapeDtypeStruct((SLOTS, fields, PB, LANES), BF16),
            jax.ShapeDtypeStruct((per_owner, fields - EARLY, PB, LANES), BF16),
        ],
        in_specs=[
            SMEM,
            SMEM,
            pl.BlockSpec((1, fine), lambda i: (0, 0)),
            pl.BlockSpec((group, fields, fine, LANES), lambda i: (i, 0, 0, 0)),
            ANY,
        ],
        out_specs=[ANY, ANY],
        scratch_shapes=[
            pltpu.VMEM((PB, fine), BF16),
            pltpu.VMEM((fields, PB, LANES), BF16),
            pltpu.VMEM((per_owner, fields, PB, LANES), BF16),
            pltpu.SemaphoreType.DMA,
            pltpu.SemaphoreType.DMA,
        ],
        compiler_params=PARAMS,
        cost_estimate=cost(fields * 2**22, 2 * per_owner * fields * PB * fine * LANES),
    )(slot, has_patch, fine_map.reshape(1, fine), fine_cells, after)


def local_kernel(z_ref, late_ref, first_ref, patches_ref, coarse_ref, *rest):
    *outs, stay_ref, stage, stay, into, away, stay_sem = rest
    own = patches_ref.shape[0] // NZ
    for n, r in enumerate(SEND_ORDER):
        for j in range(QUARTER):
            box = jnp.maximum(late_ref[r * QUARTER + j], 0)
            pltpu.make_async_copy(coarse_ref.at[pl.ds(EARLY, F - EARLY), box], stage.at[n, j], into.at[n]).start()
        share = pl.ds((z_ref[0] + r) % NZ * own, own)
        pltpu.make_async_copy(patches_ref.at[share], stage.at[n, pl.ds(QUARTER, own)], into.at[n]).start()
    for j in range(QUARTER):
        pltpu.make_async_copy(coarse_ref.at[:, first_ref[j]], stay.at[j], stay_sem.at[0]).start()
    for n, r in enumerate(SEND_ORDER):
        pltpu.make_async_copy(outs[r], stage.at[n], into.at[n]).wait()
        for j in range(QUARTER):

            @pl.when(late_ref[r * QUARTER + j] < 0)
            def _(n=n, j=j):
                stage[n, j] = jnp.zeros_like(stage[n, j])

        pltpu.make_async_copy(stage.at[n], outs[r], away.at[n]).start()
    pltpu.make_async_copy(stay_ref, stay, stay_sem.at[0]).wait()
    pltpu.make_async_copy(stay, stay_ref, stay_sem.at[1]).start()
    for n, r in enumerate(SEND_ORDER):
        pltpu.make_async_copy(stage.at[n], outs[r], away.at[n]).wait()
    pltpu.make_async_copy(stay, stay_ref, stay_sem.at[1]).wait()


def local_part(z, late, first, patches, coarse):
    shape = (QUARTER + patches.shape[0] // NZ, patches.shape[1], PB, LANES)
    stay = (QUARTER, F, PB, LANES)
    return pl.pallas_call(
        local_kernel,
        out_shape=[jax.ShapeDtypeStruct(shape, BF16)] * NZ + [jax.ShapeDtypeStruct(stay, BF16)],
        in_specs=[SMEM, SMEM, SMEM, ANY, ANY],
        out_specs=[ANY] * (NZ + 1),
        scratch_shapes=[
            pltpu.VMEM((NZ, *shape), BF16),
            pltpu.VMEM(stay, BF16),
            pltpu.SemaphoreType.DMA((NZ,)),
            pltpu.SemaphoreType.DMA((NZ,)),
            pltpu.SemaphoreType.DMA((2,)),
        ],
        compiler_params=PARAMS,
        cost_estimate=cost(2**22),
    )(z, late, first, patches, coarse)


def merge_kernel(order_ref, pick_ref, received_ref, coarse_ref, after_ref, *rest):
    outs, (stage, into, away) = rest[:-3], rest[-3:]
    fields = pl.ds(0, EARLY)
    for n, r in enumerate(SEND_ORDER):
        for j in range(QUARTER):
            k = r * QUARTER + j
            box = pick_ref[k]

            @pl.when(box < 0)
            def _(n=n, j=j, k=k):
                pltpu.make_async_copy(received_ref.at[order_ref[k], fields], stage.at[n, j], into.at[n]).start()

            @pl.when(box >= 0)
            def _(n=n, j=j, box=box):
                pltpu.make_async_copy(coarse_ref.at[fields, box], stage.at[n, j], into.at[n]).start()

    stage_out(stage, [outs[r] for r in SEND_ORDER], into, away)


def merge(order, pick, received, coarse, after):
    shape = (QUARTER, EARLY, PB, LANES)
    return pl.pallas_call(
        merge_kernel,
        out_shape=[jax.ShapeDtypeStruct(shape, BF16)] * NZ,
        in_specs=[SMEM, SMEM, ANY, ANY, ANY],
        out_specs=[ANY] * NZ,
        scratch_shapes=[pltpu.VMEM((NZ, *shape), BF16)] + [pltpu.SemaphoreType.DMA((NZ,))] * 2,
        compiler_params=PARAMS,
        cost_estimate=cost(4 * 2**20),
    )(order, pick, received, coarse, after)


def output_kernel(slots_ref, out_ref, stage, into, away):
    ins = [pltpu.make_async_copy(slots_ref.at[:, f], stage.at[f], into.at[f]) for f in range(F)]
    outs = [pltpu.make_async_copy(stage.at[f], out_ref.at[f], away.at[f]) for f in range(F)]
    for copy in ins:
        copy.start()
    for copy, out in zip(ins, outs):
        copy.wait()
        out.start()
    for out in outs:
        out.wait()


def slot_output(slots):
    return pl.pallas_call(
        output_kernel,
        out_shape=jax.ShapeDtypeStruct((F, SLOTS, PB, LANES), BF16),
        in_specs=[ANY],
        out_specs=ANY,
        scratch_shapes=[pltpu.VMEM((F, SLOTS, PB, LANES), BF16)] + [pltpu.SemaphoreType.DMA((F,))] * 2,
        compiler_params=PARAMS,
        cost_estimate=cost(8 * 2**20),
    )(slots)


def gram_kernel(offset, has_before, scale, weight_ref, z_ref, x0, x1, x2, x3, *rest):
    f = pl.program_id(0)
    before_ref, out_ref, total = rest[0], rest[-1 if scale is None else -2], rest[-1]

    @pl.when(f == 0)
    def _():
        total[...] = before_ref[...] if has_before else jnp.zeros_like(total)

    cells = x0.shape[0] * PB
    wide = jnp.concatenate([x[...].reshape(cells, LANES) for x in (x0, x1, x2, x3)], axis=1)
    product = lax.dot_general(wide, wide, (((0,), (0,)), ((), ())), preferred_element_type=F32)
    for b in range(NZ):
        total[b] += weight_ref[offset + f] * product[:, b * LANES : (b + 1) * LANES]

    if scale is not None:

        @pl.when(f == pl.num_programs(0) - 1)
        def _():
            z = z_ref[0]
            rows = S // 128
            for a in range(NZ):
                ga = (GRAM_ORDER[a] + z) % NZ
                for b in range(NZ):
                    gb = (GRAM_ORDER[b] + z) % NZ
                    for i in range(rows):
                        part = total[b, pl.ds(a * LANES + i, LANES // rows, stride=rows), :]
                        start = ga * (LANES // rows) * 16 + gb * rows + i
                        out_ref[pl.ds(start, LANES // rows, stride=16), :] = part * scale


def gram(weight, z, xs, before=None, offset=0, scale=None, effort=1, after=None):
    boxes, fields = xs[0].shape[:2]
    block = pl.BlockSpec((boxes, 1, PB, LANES), lambda f: (0, f, 0, 0))
    whole = pl.BlockSpec((NZ, S, LANES), lambda f: (0, 0, 0))
    more = [] if before is None else [(before, whole)]
    if after is not None:
        more.append((after, ANY))
    last = scale is not None
    return pl.pallas_call(
        lambda *refs: gram_kernel(offset, before is not None, scale, *refs),
        grid=(fields,),
        out_shape=jax.ShapeDtypeStruct((S * NZ, LANES) if last else (NZ, S, LANES), F32),
        in_specs=[SMEM, SMEM] + [block] * NZ + [spec for _, spec in more],
        out_specs=pl.BlockSpec((S * NZ, LANES), lambda f: (0, 0)) if last else whole,
        scratch_shapes=[pltpu.VMEM((NZ, S, LANES), F32)] if last else [],
        compiler_params=PARAMS,
        cost_estimate=cost(effort * (fields * 2**20 + 2**21), effort * 2 * fields * boxes * PB * S * S),
    )(weight, z, *xs, *[x for x, _ in more])


def shift(x, by):
    return lax.ppermute(x, "snap", [(i, (i + by) % NZ) for i in range(NZ)])


def exchange(sends):
    return tuple(shift(sends[(NZ - g) % NZ], (NZ - g) % NZ) if g else sends[0] for g in GRAM_ORDER)


def anchor(*behind):
    def kernel(*refs):
        refs[-1][...] = jnp.zeros_like(refs[-1])

    return pl.pallas_call(
        kernel,
        out_shape=jax.ShapeDtypeStruct((8, LANES), F32),
        in_specs=[ANY] * len(behind),
        out_specs=VMEM,
        compiler_params=PARAMS,
        cost_estimate=cost(2**30, 2**40),
    )(*behind)


def on_device(coarse, fine_cells, patch_block, fine_map, field_weight):
    own = lax.axis_index(XY).astype(I32)
    z = lax.axis_index("snap").astype(I32)
    per_owner = fine_cells.shape[0]
    blocks_dev = coarse.shape[1] // PB
    coarse_boxes = coarse.reshape(F, blocks_dev, PB, LANES)
    first, slot, has_patch, order, pick, late = tables(patch_block, own, z, per_owner, blocks_dev)
    at_z = z.reshape(1)

    (across,) = gather_free(first, coarse_boxes, (2,), field_weight)
    outgoing, patches = restrict(slot, has_patch, fine_map, fine_cells, across)
    up, down = gather_free(first, coarse_boxes, (1, 3), patches)
    received = lax.all_to_all(outgoing, XY, split_axis=0, concat_axis=0, tiled=True)
    *local_sends, stay = local_part(at_z, late, first, patches, coarse_boxes)
    free = exchange((stay, up, across, down))
    local = exchange(local_sends)

    slots = exchange(merge(order, pick, received, coarse_boxes, anchor(free[1], local_sends[0])))
    total = gram(field_weight, at_z, free, effort=400)
    total = gram(field_weight, at_z, local, total, EARLY, effort=400)

    scale = 1.0 / (F * coarse.shape[1] * OWNERS)
    shares = gram(field_weight, at_z, slots, total, 0, scale)

    collected = lax.all_to_all(shares, ALL, split_axis=0, concat_axis=0, tiled=True)
    restricted = slot_output(received)
    summed = jnp.sum(collected.reshape(128, NZ, NZ, LANES), axis=0)
    gram_matrix = summed.transpose(1, 0, 2).reshape(S // 128, S)
    return (gram_matrix, restricted)


def solution(mesh):
    return jax.shard_map(
        on_device,
        mesh=mesh,
        in_specs=(
            P(None, ("tile", "level"), "snap"),
            P(("tile", "level"), None, None, "snap"),
            P(),
            P(),
            P(),
        ),
        out_specs=(P(("snap", "tile", "level"), None), P(None, ("tile", "level"), None, "snap")),
        check_vma=False,
    )
```

```python
import jax
import jax.numpy as jnp
from jax import lax
from jax.experimental import pallas as pl
from jax.experimental.pallas import tpu as pltpu
from jax.sharding import PartitionSpec as P

F = 4
PB = 64
SLOTS = 64
NZ = 4
OWNERS = 32
LANES = 128
QUARTER = SLOTS // NZ
EARLY = 2
S = NZ * LANES
SEND_ORDER = (2, 1, 3, 0)
GRAM_ORDER = (0, 2, 1, 3)
XY = ("tile", "level")
ALL = ("snap", "tile", "level")
BF16, F32, I32 = jnp.bfloat16, jnp.float32, jnp.int32
ANY = pl.BlockSpec(memory_space=pl.ANY)
SMEM = pl.BlockSpec(memory_space=pltpu.SMEM)
VMEM = pl.BlockSpec(memory_space=pltpu.VMEM)
PARAMS = pltpu.CompilerParams(vmem_limit_bytes=58 * 2**20)


def cost(bytes_accessed, flops=0):
    return pl.CostEstimate(flops=flops, bytes_accessed=bytes_accessed, transcendentals=0)


def free_boxes(patch_block, own, z, blocks_dev):
    k = jnp.arange(SLOTS, dtype=I32)
    order = QUARTER * ((z + k // QUARTER) % NZ) + k % QUARTER
    boxes = jnp.arange(blocks_dev, dtype=I32)
    local = patch_block - own * blocks_dev
    free = jnp.all(local[None, :] != boxes[:, None], axis=1)
    rank_free = jnp.sum((free[None, :] & (boxes[None, :] < boxes[:, None])).astype(I32), axis=1)
    place = jnp.where(free, rank_free, -1)
    first = jnp.sum(jnp.where(place[None, :] == order[:, None], boxes[None, :], 0), axis=1)
    return order, place, first


def tables(patch_block, own, order, place, per_owner, blocks_dev):
    k = jnp.arange(SLOTS, dtype=I32)
    boxes = jnp.arange(blocks_dev, dtype=I32)
    target = lax.shift_right_logical(patch_block, jnp.int32(blocks_dev.bit_length() - 1))
    own_target = lax.dynamic_slice_in_dim(target, own * per_owner, per_owner)
    p = jnp.arange(per_owner, dtype=I32)
    same = (own_target[None, :] == own_target[:, None]) & (p[None, :] < p[:, None])
    slot = own_target * (SLOTS // OWNERS) + jnp.sum(same.astype(I32), axis=1)
    has_patch = jnp.any(slot[None, :] == k[:, None], axis=1).astype(I32)

    arrived = jnp.sum((target.reshape(OWNERS, per_owner) == own).astype(I32), axis=1)
    filled = (arrived[:, None] > jnp.arange(SLOTS // OWNERS, dtype=I32)[None, :]).reshape(SLOTS)
    empty_before = jnp.sum(((~filled)[None, :] & (k[None, :] < order[:, None])).astype(I32), axis=1)
    second = jnp.sum(jnp.where(place[None, :] == SLOTS + empty_before[:, None], boxes[None, :], 0), axis=1)
    filled_at = jnp.any(filled[None, :] & (k[None, :] == order[:, None]), axis=1)
    pick = jnp.where(filled_at, -1, second)
    late = jnp.sum(jnp.where(place[None, :] == SLOTS + order[:, None], boxes[None, :] + 1, 0), axis=1) - 1
    return slot, has_patch, pick, late


def stage_out(stage, outs, into, away):
    for n, out in enumerate(outs):
        pltpu.make_async_copy(out, stage.at[n], into.at[n]).wait()
        pltpu.make_async_copy(stage.at[n], out, away.at[n]).start()
    for n, out in enumerate(outs):
        pltpu.make_async_copy(stage.at[n], out, away.at[n]).wait()


def gather_kernel(parts, first_ref, coarse_ref, after_ref, *rest):
    outs, (stage, into, away) = rest[:-3], rest[-3:]
    for n, r in enumerate(parts):
        for j in range(QUARTER):
            pltpu.make_async_copy(coarse_ref.at[:, first_ref[r * QUARTER + j]], stage.at[n, j], into.at[n]).start()
    stage_out(stage, outs, into, away)


def gather_free(first, coarse, parts, after):
    shape = (QUARTER, F, PB, LANES)
    return pl.pallas_call(
        lambda *refs: gather_kernel(parts, *refs),
        out_shape=[jax.ShapeDtypeStruct(shape, BF16) for _ in parts],
        in_specs=[SMEM, ANY, ANY],
        out_specs=[ANY for _ in parts],
        scratch_shapes=[pltpu.VMEM((len(parts), *shape), BF16)] + [pltpu.SemaphoreType.DMA((NZ,))] * 2,
        compiler_params=PARAMS,
        cost_estimate=cost(2 * len(parts) * QUARTER * F * PB * LANES * 2),
    )(first, coarse, after)


def restrict_kernel(steps, group, fields, slot_ref, has_ref, map_ref, fine_ref, after_ref, out_ref, plain_ref, averaging, zeros, results, sem, plain_sem):
    step = pl.program_id(0)

    @pl.when(step == 0)
    def _():
        e_of = map_ref[...]
        b = lax.broadcasted_iota(I32, averaging.shape, 0)
        averaging[...] = jnp.where(e_of == b, 0.125, 0.0).astype(BF16)
        zeros[...] = jnp.zeros_like(zeros)
        for q in range(SLOTS):

            @pl.when(has_ref[q] == 0)
            def _(q=q):
                pltpu.make_async_copy(zeros, out_ref.at[q], sem).start()

    for i in range(group):
        p = step * group + i
        wide = jnp.concatenate([fine_ref[i, f] for f in range(fields)], axis=1)
        mean = jnp.dot(averaging[...], wide, preferred_element_type=F32).astype(BF16)
        for f in range(fields):
            results[p, f] = mean[:, f * LANES : (f + 1) * LANES]
        pltpu.make_async_copy(results.at[p], out_ref.at[slot_ref[p]], sem).start()

    @pl.when(step == steps - 1)
    def _():
        plain = pltpu.make_async_copy(results.at[:, pl.ds(EARLY, fields - EARLY)], plain_ref, plain_sem)
        plain.start()
        plain.wait()
        pltpu.make_async_copy(out_ref, out_ref, sem).wait()


def restrict(slot, has_patch, fine_map, fine_cells, after):
    per_owner, fields, fine, _ = fine_cells.shape
    group = 4
    steps = per_owner // group
    return pl.pallas_call(
        lambda *refs: restrict_kernel(steps, group, fields, *refs),
        grid=(steps,),
        out_shape=[
            jax.ShapeDtypeStruct((SLOTS, fields, PB, LANES), BF16),
            jax.ShapeDtypeStruct((per_owner, fields - EARLY, PB, LANES), BF16),
        ],
        in_specs=[
            SMEM,
            SMEM,
            pl.BlockSpec((1, fine), lambda i: (0, 0)),
            pl.BlockSpec((group, fields, fine, LANES), lambda i: (i, 0, 0, 0)),
            ANY,
        ],
        out_specs=[ANY, ANY],
        scratch_shapes=[
            pltpu.VMEM((PB, fine), BF16),
            pltpu.VMEM((fields, PB, LANES), BF16),
            pltpu.VMEM((per_owner, fields, PB, LANES), BF16),
            pltpu.SemaphoreType.DMA,
            pltpu.SemaphoreType.DMA,
        ],
        compiler_params=PARAMS,
        cost_estimate=cost(fields * 2**22, 2 * per_owner * fields * PB * fine * LANES),
    )(slot, has_patch, fine_map.reshape(1, fine), fine_cells, after)


def local_kernel(z_ref, late_ref, first_ref, patches_ref, coarse_ref, *rest):
    *outs, stay_ref, stage, stay, into, away, stay_sem = rest
    own = patches_ref.shape[0] // NZ
    for n, r in enumerate(SEND_ORDER):
        for j in range(QUARTER):
            box = jnp.maximum(late_ref[r * QUARTER + j], 0)
            pltpu.make_async_copy(coarse_ref.at[pl.ds(EARLY, F - EARLY), box], stage.at[n, j], into.at[n]).start()
        share = pl.ds((z_ref[0] + r) % NZ * own, own)
        pltpu.make_async_copy(patches_ref.at[share], stage.at[n, pl.ds(QUARTER, own)], into.at[n]).start()
    for j in range(QUARTER):
        pltpu.make_async_copy(coarse_ref.at[:, first_ref[j]], stay.at[j], stay_sem.at[0]).start()
    for n, r in enumerate(SEND_ORDER):
        pltpu.make_async_copy(outs[r], stage.at[n], into.at[n]).wait()
        for j in range(QUARTER):

            @pl.when(late_ref[r * QUARTER + j] < 0)
            def _(n=n, j=j):
                stage[n, j] = jnp.zeros_like(stage[n, j])

        pltpu.make_async_copy(stage.at[n], outs[r], away.at[n]).start()
    pltpu.make_async_copy(stay_ref, stay, stay_sem.at[0]).wait()
    pltpu.make_async_copy(stay, stay_ref, stay_sem.at[1]).start()
    for n, r in enumerate(SEND_ORDER):
        pltpu.make_async_copy(stage.at[n], outs[r], away.at[n]).wait()
    pltpu.make_async_copy(stay, stay_ref, stay_sem.at[1]).wait()


def local_part(z, late, first, patches, coarse):
    shape = (QUARTER + patches.shape[0] // NZ, patches.shape[1], PB, LANES)
    stay = (QUARTER, F, PB, LANES)
    return pl.pallas_call(
        local_kernel,
        out_shape=[jax.ShapeDtypeStruct(shape, BF16)] * NZ + [jax.ShapeDtypeStruct(stay, BF16)],
        in_specs=[SMEM, SMEM, SMEM, ANY, ANY],
        out_specs=[ANY] * (NZ + 1),
        scratch_shapes=[
            pltpu.VMEM((NZ, *shape), BF16),
            pltpu.VMEM(stay, BF16),
            pltpu.SemaphoreType.DMA((NZ,)),
            pltpu.SemaphoreType.DMA((NZ,)),
            pltpu.SemaphoreType.DMA((2,)),
        ],
        compiler_params=PARAMS,
        cost_estimate=cost(2**22),
    )(z, late, first, patches, coarse)


def merge_kernel(order_ref, pick_ref, received_ref, coarse_ref, after_ref, *rest):
    outs, (stage, into, away) = rest[:-3], rest[-3:]
    fields = pl.ds(0, EARLY)
    for n, r in enumerate(SEND_ORDER):
        for j in range(QUARTER):
            k = r * QUARTER + j
            box = pick_ref[k]

            @pl.when(box < 0)
            def _(n=n, j=j, k=k):
                pltpu.make_async_copy(received_ref.at[order_ref[k], fields], stage.at[n, j], into.at[n]).start()

            @pl.when(box >= 0)
            def _(n=n, j=j, box=box):
                pltpu.make_async_copy(coarse_ref.at[fields, box], stage.at[n, j], into.at[n]).start()

    stage_out(stage, [outs[r] for r in SEND_ORDER], into, away)


def merge(order, pick, received, coarse, after):
    shape = (QUARTER, EARLY, PB, LANES)
    return pl.pallas_call(
        merge_kernel,
        out_shape=[jax.ShapeDtypeStruct(shape, BF16)] * NZ,
        in_specs=[SMEM, SMEM, ANY, ANY, ANY],
        out_specs=[ANY] * NZ,
        scratch_shapes=[pltpu.VMEM((NZ, *shape), BF16)] + [pltpu.SemaphoreType.DMA((NZ,))] * 2,
        compiler_params=PARAMS,
        cost_estimate=cost(4 * 2**20),
    )(order, pick, received, coarse, after)


def output_kernel(slots_ref, out_ref, stage, into, away):
    ins = [pltpu.make_async_copy(slots_ref.at[:, f], stage.at[f], into.at[f]) for f in range(F)]
    outs = [pltpu.make_async_copy(stage.at[f], out_ref.at[f], away.at[f]) for f in range(F)]
    for copy in ins:
        copy.start()
    for copy, out in zip(ins, outs):
        copy.wait()
        out.start()
    for out in outs:
        out.wait()


def slot_output(slots):
    return pl.pallas_call(
        output_kernel,
        out_shape=jax.ShapeDtypeStruct((F, SLOTS, PB, LANES), BF16),
        in_specs=[ANY],
        out_specs=ANY,
        scratch_shapes=[pltpu.VMEM((F, SLOTS, PB, LANES), BF16)] + [pltpu.SemaphoreType.DMA((F,))] * 2,
        compiler_params=PARAMS,
        cost_estimate=cost(8 * 2**20),
    )(slots)


def gram_kernel(offset, has_before, scale, weight_ref, place_ref, x0, x1, x2, x3, *rest):
    f = pl.program_id(0)
    before_ref, total = rest[0], rest[-1]

    @pl.when(f == 0)
    def _():
        total[...] = before_ref[...] if has_before else jnp.zeros_like(total)

    cells = x0.shape[0] * PB
    wide = jnp.concatenate([x[...].reshape(cells, LANES) for x in (x0, x1, x2, x3)], axis=1)
    product = lax.dot_general(wide, wide, (((0,), (0,)), ((), ())), preferred_element_type=F32)
    for b in range(NZ):
        total[b] += weight_ref[offset + f] * product[:, b * LANES : (b + 1) * LANES]

    if scale is not None:

        @pl.when(f == pl.num_programs(0) - 1)
        def _():
            for level in range(2):

                @pl.when(place_ref[1] == level)
                def _(level=level):
                    split_pieces(place_ref[0], total, scale, rest[-3], rest[-2], level)


def split_pieces(z, total, scale, keep_ref, send_ref, level):
    rows = 4
    per_group = LANES // (2 * rows)
    for a in range(NZ):
        ga = (GRAM_ORDER[a] + z) % NZ
        for b in range(NZ):
            gb = (GRAM_ORDER[b] + z) % NZ
            for half in range(2):
                out_ref = keep_ref if half == level else send_ref
                for i in range(rows):
                    part = total[b, pl.ds(a * LANES + half * rows + i, per_group, stride=2 * rows), :]
                    start = ga * per_group * NZ * rows + gb * rows + i
                    out_ref[pl.ds(start, per_group, stride=NZ * rows), :] = part * scale


def gram(weight, place, xs, before=None, offset=0, scale=None, effort=1, after=None):
    boxes, fields = xs[0].shape[:2]
    block = pl.BlockSpec((boxes, 1, PB, LANES), lambda f: (0, f, 0, 0))
    whole = pl.BlockSpec((NZ, S, LANES), lambda f: (0, 0, 0))
    more = [] if before is None else [(before, whole)]
    if after is not None:
        more.append((after, ANY))
    last = scale is not None
    return pl.pallas_call(
        lambda *refs: gram_kernel(offset, before is not None, scale, *refs),
        grid=(fields,),
        out_shape=[jax.ShapeDtypeStruct((S * NZ // 2, LANES), F32)] * 2 if last else jax.ShapeDtypeStruct((NZ, S, LANES), F32),
        in_specs=[SMEM, SMEM] + [block] * NZ + [spec for _, spec in more],
        out_specs=[pl.BlockSpec((S * NZ // 2, LANES), lambda f: (0, 0))] * 2 if last else whole,
        scratch_shapes=[pltpu.VMEM((NZ, S, LANES), F32)] if last else [],
        compiler_params=PARAMS,
        cost_estimate=cost(effort * (fields * 2**20 + 2**21), effort * 2 * fields * boxes * PB * S * S),
    )(weight, place, *xs, *[x for x, _ in more])


def shift(x, by):
    return lax.ppermute(x, "snap", [(i, (i + by) % NZ) for i in range(NZ)])


def exchange(sends):
    return tuple(shift(sends[(NZ - g) % NZ], (NZ - g) % NZ) if g else sends[0] for g in GRAM_ORDER)


def anchor(*behind):
    def kernel(*refs):
        refs[-1][...] = jnp.zeros_like(refs[-1])

    return pl.pallas_call(
        kernel,
        out_shape=jax.ShapeDtypeStruct((8, LANES), F32),
        in_specs=[ANY] * len(behind),
        out_specs=VMEM,
        compiler_params=PARAMS,
        cost_estimate=cost(2**30, 2**40),
    )(*behind)


def on_device(coarse, fine_cells, patch_block, fine_map, field_weight):
    own = lax.axis_index(XY).astype(I32)
    z = lax.axis_index("snap").astype(I32)
    per_owner = fine_cells.shape[0]
    blocks_dev = coarse.shape[1] // PB
    coarse_boxes = coarse.reshape(F, blocks_dev, PB, LANES)
    order, place, first = free_boxes(patch_block, own, z, blocks_dev)
    at_z = z.reshape(1)
    spot = jnp.stack([z, lax.axis_index("level").astype(I32)])

    (across,) = gather_free(first, coarse_boxes, (2,), field_weight)
    patch_block, across = lax.optimization_barrier((patch_block, across))
    slot, has_patch, pick, late = tables(patch_block, own, order, place, per_owner, blocks_dev)
    outgoing, patches = restrict(slot, has_patch, fine_map, fine_cells, across)
    up, down = gather_free(first, coarse_boxes, (1, 3), patches)
    received = lax.all_to_all(outgoing, XY, split_axis=0, concat_axis=0, tiled=True)
    *local_sends, stay = local_part(at_z, late, first, patches, coarse_boxes)
    free = exchange((stay, up, across, down))
    local = exchange(local_sends)

    slots = exchange(merge(order, pick, received, coarse_boxes, anchor(free[1], local_sends[0])))
    total = gram(field_weight, spot, free, effort=400)
    total = gram(field_weight, spot, local, total, EARLY, effort=400)

    scale = 1.0 / (F * coarse.shape[1] * OWNERS)
    keep, send = gram(field_weight, spot, slots, total, 0, scale)

    shares = keep + lax.ppermute(send, "level", [(0, 1), (1, 0)])
    collected = lax.all_to_all(shares, ("snap", "tile"), split_axis=0, concat_axis=0, tiled=True)
    restricted = slot_output(received)
    summed = jnp.sum(collected.reshape(S // 8, NZ, NZ, LANES), axis=0)
    gram_matrix = summed.transpose(1, 0, 2).reshape(S // 128, S)
    return (gram_matrix, restricted)


def solution(mesh):
    return jax.shard_map(
        on_device,
        mesh=mesh,
        in_specs=(
            P(None, ("tile", "level"), "snap"),
            P(("tile", "level"), None, None, "snap"),
            P(),
            P(),
            P(),
        ),
        out_specs=(P(("snap", "tile", "level"), None), P(None, ("tile", "level"), None, "snap")),
        check_vma=False,
    )
```

```python
import jax
import jax.numpy as jnp
from jax import lax
from jax.experimental import pallas as pl
from jax.experimental.pallas import tpu as pltpu
from jax.sharding import PartitionSpec as P

F = 4
PB = 64
SLOTS = 64
NZ = 4
OWNERS = 32
LANES = 128
QUARTER = SLOTS // NZ
EARLY = 2
S = NZ * LANES
SEND_ORDER = (2, 1, 3, 0)
GRAM_ORDER = (0, 2, 1, 3)
XY = ("tile", "level")
ALL = ("snap", "tile", "level")
BF16, F32, I32 = jnp.bfloat16, jnp.float32, jnp.int32
ANY = pl.BlockSpec(memory_space=pl.ANY)
SMEM = pl.BlockSpec(memory_space=pltpu.SMEM)
VMEM = pl.BlockSpec(memory_space=pltpu.VMEM)
PARAMS = pltpu.CompilerParams(vmem_limit_bytes=58 * 2**20)
SMALL = pltpu.CompilerParams(vmem_limit_bytes=24 * 2**20)


def cost(bytes_accessed, flops=0):
    return pl.CostEstimate(flops=flops, bytes_accessed=bytes_accessed, transcendentals=0)


def free_boxes(patch_block, own, z, blocks_dev):
    k = jnp.arange(SLOTS, dtype=I32)
    order = QUARTER * ((z + k // QUARTER) % NZ) + k % QUARTER
    boxes = jnp.arange(blocks_dev, dtype=I32)
    local = patch_block - own * blocks_dev
    free = jnp.all(local[None, :] != boxes[:, None], axis=1)
    rank_free = jnp.sum((free[None, :] & (boxes[None, :] < boxes[:, None])).astype(I32), axis=1)
    place = jnp.where(free, rank_free, -1)
    first = jnp.sum(jnp.where(place[None, :] == order[:, None], boxes[None, :], 0), axis=1)
    return order, place, first


def tables(patch_block, own, order, place, per_owner, blocks_dev):
    k = jnp.arange(SLOTS, dtype=I32)
    boxes = jnp.arange(blocks_dev, dtype=I32)
    target = lax.shift_right_logical(patch_block, jnp.int32(blocks_dev.bit_length() - 1))
    own_target = lax.dynamic_slice_in_dim(target, own * per_owner, per_owner)
    p = jnp.arange(per_owner, dtype=I32)
    same = (own_target[None, :] == own_target[:, None]) & (p[None, :] < p[:, None])
    slot = own_target * (SLOTS // OWNERS) + jnp.sum(same.astype(I32), axis=1)
    has_patch = jnp.any(slot[None, :] == k[:, None], axis=1).astype(I32)

    arrived = jnp.sum((target.reshape(OWNERS, per_owner) == own).astype(I32), axis=1)
    filled = (arrived[:, None] > jnp.arange(SLOTS // OWNERS, dtype=I32)[None, :]).reshape(SLOTS)
    empty_before = jnp.sum(((~filled)[None, :] & (k[None, :] < order[:, None])).astype(I32), axis=1)
    second = jnp.sum(jnp.where(place[None, :] == SLOTS + empty_before[:, None], boxes[None, :], 0), axis=1)
    filled_at = jnp.any(filled[None, :] & (k[None, :] == order[:, None]), axis=1)
    pick = jnp.where(filled_at, -1, second)
    late = jnp.sum(jnp.where(place[None, :] == SLOTS + order[:, None], boxes[None, :] + 1, 0), axis=1) - 1
    return slot, has_patch, pick, late


def stage_out(stage, outs, into, away):
    for n, out in enumerate(outs):
        pltpu.make_async_copy(out, stage.at[n], into.at[n]).wait()
        pltpu.make_async_copy(stage.at[n], out, away.at[n]).start()
    for n, out in enumerate(outs):
        pltpu.make_async_copy(stage.at[n], out, away.at[n]).wait()


def gather_kernel(parts, first_ref, coarse_ref, after_ref, *rest):
    outs, (stage, into, away) = rest[:-3], rest[-3:]
    for n, r in enumerate(parts):
        for j in range(QUARTER):
            pltpu.make_async_copy(coarse_ref.at[:, first_ref[r * QUARTER + j]], stage.at[n, j], into.at[n]).start()
    stage_out(stage, outs, into, away)


def gather_free(first, coarse, parts, after):
    shape = (QUARTER, F, PB, LANES)
    return pl.pallas_call(
        lambda *refs: gather_kernel(parts, *refs),
        out_shape=[jax.ShapeDtypeStruct(shape, BF16) for _ in parts],
        in_specs=[SMEM, ANY, ANY],
        out_specs=[ANY for _ in parts],
        scratch_shapes=[pltpu.VMEM((len(parts), *shape), BF16)] + [pltpu.SemaphoreType.DMA((NZ,))] * 2,
        compiler_params=PARAMS,
        cost_estimate=cost(2 * len(parts) * QUARTER * F * PB * LANES * 2),
    )(first, coarse, after)


def restrict_kernel(steps, group, fields, slot_ref, has_ref, map_ref, fine_ref, after_ref, out_ref, plain_ref, averaging, zeros, results, sem, plain_sem):
    step = pl.program_id(0)

    @pl.when(step == 0)
    def _():
        e_of = map_ref[...]
        b = lax.broadcasted_iota(I32, averaging.shape, 0)
        averaging[...] = jnp.where(e_of == b, 0.125, 0.0).astype(BF16)
        zeros[...] = jnp.zeros_like(zeros)
        for q in range(SLOTS):

            @pl.when(has_ref[q] == 0)
            def _(q=q):
                pltpu.make_async_copy(zeros, out_ref.at[q], sem).start()

    for i in range(group):
        p = step * group + i
        wide = jnp.concatenate([fine_ref[i, f] for f in range(fields)], axis=1)
        mean = jnp.dot(averaging[...], wide, preferred_element_type=F32).astype(BF16)
        for f in range(fields):
            results[p, f] = mean[:, f * LANES : (f + 1) * LANES]
        pltpu.make_async_copy(results.at[p], out_ref.at[slot_ref[p]], sem).start()

    @pl.when(step == steps - 1)
    def _():
        plain = pltpu.make_async_copy(results.at[:, pl.ds(EARLY, fields - EARLY)], plain_ref, plain_sem)
        plain.start()
        plain.wait()
        pltpu.make_async_copy(out_ref, out_ref, sem).wait()


def restrict(slot, has_patch, fine_map, fine_cells, after):
    per_owner, fields, fine, _ = fine_cells.shape
    group = 4
    steps = per_owner // group
    return pl.pallas_call(
        lambda *refs: restrict_kernel(steps, group, fields, *refs),
        grid=(steps,),
        out_shape=[
            jax.ShapeDtypeStruct((SLOTS, fields, PB, LANES), BF16),
            jax.ShapeDtypeStruct((per_owner, fields - EARLY, PB, LANES), BF16),
        ],
        in_specs=[
            SMEM,
            SMEM,
            pl.BlockSpec((1, fine), lambda i: (0, 0)),
            pl.BlockSpec((group, fields, fine, LANES), lambda i: (i, 0, 0, 0)),
            ANY,
        ],
        out_specs=[ANY, ANY],
        scratch_shapes=[
            pltpu.VMEM((PB, fine), BF16),
            pltpu.VMEM((fields, PB, LANES), BF16),
            pltpu.VMEM((per_owner, fields, PB, LANES), BF16),
            pltpu.SemaphoreType.DMA,
            pltpu.SemaphoreType.DMA,
        ],
        compiler_params=PARAMS,
        cost_estimate=cost(fields * 2**22, 2 * per_owner * fields * PB * fine * LANES),
    )(slot, has_patch, fine_map.reshape(1, fine), fine_cells, after)


def local_kernel(z_ref, late_ref, first_ref, patches_ref, coarse_ref, *rest):
    *outs, stay_ref, stage, stay, into, away, stay_sem = rest
    own = patches_ref.shape[0] // NZ
    for n, r in enumerate(SEND_ORDER):
        for j in range(QUARTER):
            box = jnp.maximum(late_ref[r * QUARTER + j], 0)
            pltpu.make_async_copy(coarse_ref.at[pl.ds(EARLY, F - EARLY), box], stage.at[n, j], into.at[n]).start()
        share = pl.ds((z_ref[0] + r) % NZ * own, own)
        pltpu.make_async_copy(patches_ref.at[share], stage.at[n, pl.ds(QUARTER, own)], into.at[n]).start()
    for j in range(QUARTER):
        pltpu.make_async_copy(coarse_ref.at[:, first_ref[j]], stay.at[j], stay_sem.at[0]).start()
    for n, r in enumerate(SEND_ORDER):
        pltpu.make_async_copy(outs[r], stage.at[n], into.at[n]).wait()
        for j in range(QUARTER):

            @pl.when(late_ref[r * QUARTER + j] < 0)
            def _(n=n, j=j):
                stage[n, j] = jnp.zeros_like(stage[n, j])

        pltpu.make_async_copy(stage.at[n], outs[r], away.at[n]).start()
    pltpu.make_async_copy(stay_ref, stay, stay_sem.at[0]).wait()
    pltpu.make_async_copy(stay, stay_ref, stay_sem.at[1]).start()
    for n, r in enumerate(SEND_ORDER):
        pltpu.make_async_copy(stage.at[n], outs[r], away.at[n]).wait()
    pltpu.make_async_copy(stay, stay_ref, stay_sem.at[1]).wait()


def local_part(z, late, first, patches, coarse):
    shape = (QUARTER + patches.shape[0] // NZ, patches.shape[1], PB, LANES)
    stay = (QUARTER, F, PB, LANES)
    return pl.pallas_call(
        local_kernel,
        out_shape=[jax.ShapeDtypeStruct(shape, BF16)] * NZ + [jax.ShapeDtypeStruct(stay, BF16)],
        in_specs=[SMEM, SMEM, SMEM, ANY, ANY],
        out_specs=[ANY] * (NZ + 1),
        scratch_shapes=[
            pltpu.VMEM((NZ, *shape), BF16),
            pltpu.VMEM(stay, BF16),
            pltpu.SemaphoreType.DMA((NZ,)),
            pltpu.SemaphoreType.DMA((NZ,)),
            pltpu.SemaphoreType.DMA((2,)),
        ],
        compiler_params=PARAMS,
        cost_estimate=cost(2**22),
    )(z, late, first, patches, coarse)


def merge_kernel(order_ref, pick_ref, received_ref, coarse_ref, after_ref, *rest):
    outs, (stage, into, away) = rest[:-3], rest[-3:]
    fields = pl.ds(0, EARLY)
    for n, r in enumerate(SEND_ORDER):
        for j in range(QUARTER):
            k = r * QUARTER + j
            box = pick_ref[k]

            @pl.when(box < 0)
            def _(n=n, j=j, k=k):
                pltpu.make_async_copy(received_ref.at[order_ref[k], fields], stage.at[n, j], into.at[n]).start()

            @pl.when(box >= 0)
            def _(n=n, j=j, box=box):
                pltpu.make_async_copy(coarse_ref.at[fields, box], stage.at[n, j], into.at[n]).start()

    stage_out(stage, [outs[r] for r in SEND_ORDER], into, away)


def merge(order, pick, received, coarse, after):
    shape = (QUARTER, EARLY, PB, LANES)
    return pl.pallas_call(
        merge_kernel,
        out_shape=[jax.ShapeDtypeStruct(shape, BF16)] * NZ,
        in_specs=[SMEM, SMEM, ANY, ANY, ANY],
        out_specs=[ANY] * NZ,
        scratch_shapes=[pltpu.VMEM((NZ, *shape), BF16)] + [pltpu.SemaphoreType.DMA((NZ,))] * 2,
        compiler_params=PARAMS,
        cost_estimate=cost(4 * 2**20),
    )(order, pick, received, coarse, after)


def output_kernel(slots_ref, out_ref, stage, into, away):
    ins = [pltpu.make_async_copy(slots_ref.at[:, f], stage.at[f], into.at[f]) for f in range(F)]
    outs = [pltpu.make_async_copy(stage.at[f], out_ref.at[f], away.at[f]) for f in range(F)]
    for copy in ins:
        copy.start()
    for copy, out in zip(ins, outs):
        copy.wait()
        out.start()
    for out in outs:
        out.wait()


def slot_output(slots):
    return pl.pallas_call(
        output_kernel,
        out_shape=jax.ShapeDtypeStruct((F, SLOTS, PB, LANES), BF16),
        in_specs=[ANY],
        out_specs=ANY,
        scratch_shapes=[pltpu.VMEM((F, SLOTS, PB, LANES), BF16)] + [pltpu.SemaphoreType.DMA((F,))] * 2,
        compiler_params=SMALL,
        cost_estimate=cost(8 * 2**20),
    )(slots)


def gram_kernel(offset, has_before, scale, weight_ref, place_ref, x0, x1, x2, x3, *rest):
    f = pl.program_id(0)
    before_ref, total = rest[0], rest[-1]

    @pl.when(f == 0)
    def _():
        total[...] = before_ref[...] if has_before else jnp.zeros_like(total)

    cells = x0.shape[0] * PB
    wide = jnp.concatenate([x[...].reshape(cells, LANES) for x in (x0, x1, x2, x3)], axis=1)
    product = lax.dot_general(wide, wide, (((0,), (0,)), ((), ())), preferred_element_type=F32)
    for b in range(NZ):
        total[b] += weight_ref[offset + f] * product[:, b * LANES : (b + 1) * LANES]

    if scale is not None:

        @pl.when(f == pl.num_programs(0) - 1)
        def _():
            for level in range(2):

                @pl.when(place_ref[1] == level)
                def _(level=level):
                    split_pieces(place_ref[0], total, scale, rest[-3], rest[-2], level)


def split_pieces(z, total, scale, keep_ref, send_ref, level):
    rows = 4
    per_group = LANES // (2 * rows)
    for a in range(NZ):
        ga = (GRAM_ORDER[a] + z) % NZ
        for b in range(NZ):
            gb = (GRAM_ORDER[b] + z) % NZ
            for half in range(2):
                out_ref = keep_ref if half == level else send_ref
                for i in range(rows):
                    part = total[b, pl.ds(a * LANES + half * rows + i, per_group, stride=2 * rows), :]
                    start = ga * per_group * NZ * rows + gb * rows + i
                    out_ref[pl.ds(start, per_group, stride=NZ * rows), :] = part * scale


def gram(weight, place, xs, before=None, offset=0, scale=None, effort=1, after=None):
    boxes, fields = xs[0].shape[:2]
    block = pl.BlockSpec((boxes, 1, PB, LANES), lambda f: (0, f, 0, 0))
    whole = pl.BlockSpec((NZ, S, LANES), lambda f: (0, 0, 0))
    more = [] if before is None else [(before, whole)]
    if after is not None:
        more.append((after, ANY))
    last = scale is not None
    return pl.pallas_call(
        lambda *refs: gram_kernel(offset, before is not None, scale, *refs),
        grid=(fields,),
        out_shape=[jax.ShapeDtypeStruct((S * NZ // 2, LANES), F32)] * 2 if last else jax.ShapeDtypeStruct((NZ, S, LANES), F32),
        in_specs=[SMEM, SMEM] + [block] * NZ + [spec for _, spec in more],
        out_specs=[pl.BlockSpec((S * NZ // 2, LANES), lambda f: (0, 0))] * 2 if last else whole,
        scratch_shapes=[pltpu.VMEM((NZ, S, LANES), F32)] if last else [],
        compiler_params=SMALL,
        cost_estimate=cost(effort * (fields * 2**20 + 2**21), effort * 2 * fields * boxes * PB * S * S),
    )(weight, place, *xs, *[x for x, _ in more])


def shift(x, by):
    return lax.ppermute(x, "snap", [(i, (i + by) % NZ) for i in range(NZ)])


def exchange(sends):
    return tuple(shift(sends[(NZ - g) % NZ], (NZ - g) % NZ) if g else sends[0] for g in GRAM_ORDER)


def anchor(*behind):
    def kernel(*refs):
        refs[-1][...] = jnp.zeros_like(refs[-1])

    return pl.pallas_call(
        kernel,
        out_shape=jax.ShapeDtypeStruct((8, LANES), F32),
        in_specs=[ANY] * len(behind),
        out_specs=VMEM,
        compiler_params=PARAMS,
        cost_estimate=cost(2**30, 2**40),
    )(*behind)


def on_device(coarse, fine_cells, patch_block, fine_map, field_weight):
    own = lax.axis_index(XY).astype(I32)
    z = lax.axis_index("snap").astype(I32)
    per_owner = fine_cells.shape[0]
    blocks_dev = coarse.shape[1] // PB
    coarse_boxes = coarse.reshape(F, blocks_dev, PB, LANES)
    order, place, first = free_boxes(patch_block, own, z, blocks_dev)
    at_z = z.reshape(1)
    spot = jnp.stack([z, lax.axis_index("level").astype(I32)])

    (across,) = gather_free(first, coarse_boxes, (2,), field_weight)
    patch_block, across = lax.optimization_barrier((patch_block, across))
    slot, has_patch, pick, late = tables(patch_block, own, order, place, per_owner, blocks_dev)
    outgoing, patches = restrict(slot, has_patch, fine_map, fine_cells, across)
    up, down = gather_free(first, coarse_boxes, (1, 3), patches)
    received = lax.all_to_all(outgoing, XY, split_axis=0, concat_axis=0, tiled=True)
    *local_sends, stay = local_part(at_z, late, first, patches, coarse_boxes)
    free = exchange((stay, up, across, down))
    local = exchange(local_sends)

    slots = exchange(merge(order, pick, received, coarse_boxes, anchor(free[1], local_sends[0])))
    total = gram(field_weight, spot, free, effort=400)
    total = gram(field_weight, spot, local, total, EARLY, effort=400)

    scale = 1.0 / (F * coarse.shape[1] * OWNERS)
    keep, send = gram(field_weight, spot, slots, total, 0, scale)

    shares = keep + lax.ppermute(send, "level", [(0, 1), (1, 0)])
    collected = lax.all_to_all(shares, ("snap", "tile"), split_axis=0, concat_axis=0, tiled=True)
    restricted = slot_output(received)
    summed = jnp.sum(collected.reshape(S // 8, NZ, NZ, LANES), axis=0)
    gram_matrix = summed.transpose(1, 0, 2).reshape(S // 128, S)
    return (gram_matrix, restricted)


def solution(mesh):
    return jax.shard_map(
        on_device,
        mesh=mesh,
        in_specs=(
            P(None, ("tile", "level"), "snap"),
            P(("tile", "level"), None, None, "snap"),
            P(),
            P(),
            P(),
        ),
        out_specs=(P(("snap", "tile", "level"), None), P(None, ("tile", "level"), None, "snap")),
        check_vma=False,
    )
```

```python
import jax
import jax.numpy as jnp
from jax import lax
from jax.experimental import pallas as pl
from jax.experimental.pallas import tpu as pltpu
from jax.sharding import PartitionSpec as P

F = 4
PB = 64
SLOTS = 64
NZ = 4
OWNERS = 32
LANES = 128
QUARTER = SLOTS // NZ
LOT = 4
EARLY = 2
S = NZ * LANES
SEND_ORDER = (2, 1, 3, 0)
GRAM_ORDER = (0, 2, 1, 3)
XY = ("tile", "level")
ALL = ("snap", "tile", "level")
BF16, F32, I32 = jnp.bfloat16, jnp.float32, jnp.int32
ANY = pl.BlockSpec(memory_space=pl.ANY)
SMEM = pl.BlockSpec(memory_space=pltpu.SMEM)
VMEM = pl.BlockSpec(memory_space=pltpu.VMEM)
PARAMS = pltpu.CompilerParams(vmem_limit_bytes=58 * 2**20)
SMALL = pltpu.CompilerParams(vmem_limit_bytes=24 * 2**20)


def cost(bytes_accessed, flops=0):
    return pl.CostEstimate(flops=flops, bytes_accessed=bytes_accessed, transcendentals=0)


def free_boxes(patch_block, own, z, blocks_dev):
    k = jnp.arange(SLOTS, dtype=I32)
    order = QUARTER * ((z + k // QUARTER) % NZ) + k % QUARTER
    boxes = jnp.arange(blocks_dev, dtype=I32)
    local = patch_block - own * blocks_dev
    free = jnp.all(local[None, :] != boxes[:, None], axis=1)
    rank_free = jnp.sum((free[None, :] & (boxes[None, :] < boxes[:, None])).astype(I32), axis=1)
    place = jnp.where(free, rank_free, -1)
    first = jnp.sum(jnp.where(place[None, :] == order[:, None], boxes[None, :], 0), axis=1)
    return order, place, first


def tables(patch_block, own, order, place, per_owner, blocks_dev):
    k = jnp.arange(SLOTS, dtype=I32)
    boxes = jnp.arange(blocks_dev, dtype=I32)
    target = lax.shift_right_logical(patch_block, jnp.int32(blocks_dev.bit_length() - 1))
    own_target = lax.dynamic_slice_in_dim(target, own * per_owner, per_owner)
    p = jnp.arange(per_owner, dtype=I32)
    same = (own_target[None, :] == own_target[:, None]) & (p[None, :] < p[:, None])
    slot = own_target * (SLOTS // OWNERS) + jnp.sum(same.astype(I32), axis=1)
    has_patch = jnp.any(slot[None, :] == k[:, None], axis=1).astype(I32)

    arrived = jnp.sum((target.reshape(OWNERS, per_owner) == own).astype(I32), axis=1)
    filled = (arrived[:, None] > jnp.arange(SLOTS // OWNERS, dtype=I32)[None, :]).reshape(SLOTS)
    empty_before = jnp.sum(((~filled)[None, :] & (k[None, :] < order[:, None])).astype(I32), axis=1)
    second = jnp.sum(jnp.where(place[None, :] == SLOTS + empty_before[:, None], boxes[None, :], 0), axis=1)
    filled_at = jnp.any(filled[None, :] & (k[None, :] == order[:, None]), axis=1)
    pick = jnp.where(filled_at, -1, second)
    late = jnp.sum(jnp.where(place[None, :] == SLOTS + order[:, None], boxes[None, :] + 1, 0), axis=1) - 1
    return slot, has_patch, pick, late


def stage_out(stage, outs, into, away):
    lots = [(n, c, out, pl.ds(c * LOT, LOT)) for n, out in enumerate(outs) for c in range(QUARTER // LOT)]
    for n, c, out, part in lots:
        pltpu.make_async_copy(out.at[part], stage.at[n, part], into.at[n, c]).wait()
        pltpu.make_async_copy(stage.at[n, part], out.at[part], away.at[n]).start()
    for n, out in enumerate(outs):
        pltpu.make_async_copy(stage.at[n], out, away.at[n]).wait()


def gather_kernel(parts, first_ref, coarse_ref, after_ref, *rest):
    outs, (stage, into, away) = rest[:-3], rest[-3:]
    for n, r in enumerate(parts):
        for j in range(QUARTER):
            pltpu.make_async_copy(coarse_ref.at[:, first_ref[r * QUARTER + j]], stage.at[n, j], into.at[n, j // LOT]).start()
    stage_out(stage, outs, into, away)


def gather_free(first, coarse, parts, after):
    shape = (QUARTER, F, PB, LANES)
    return pl.pallas_call(
        lambda *refs: gather_kernel(parts, *refs),
        out_shape=[jax.ShapeDtypeStruct(shape, BF16) for _ in parts],
        in_specs=[SMEM, ANY, ANY],
        out_specs=[ANY for _ in parts],
        scratch_shapes=[pltpu.VMEM((len(parts), *shape), BF16)] + [pltpu.SemaphoreType.DMA((NZ, QUARTER // LOT)), pltpu.SemaphoreType.DMA((NZ,))],
        compiler_params=PARAMS,
        cost_estimate=cost(2 * len(parts) * QUARTER * F * PB * LANES * 2),
    )(first, coarse, after)


def restrict_kernel(steps, group, fields, slot_ref, has_ref, map_ref, fine_ref, after_ref, out_ref, plain_ref, averaging, zeros, results, sem, plain_sem):
    step = pl.program_id(0)

    @pl.when(step == 0)
    def _():
        e_of = map_ref[...]
        b = lax.broadcasted_iota(I32, averaging.shape, 0)
        averaging[...] = jnp.where(e_of == b, 0.125, 0.0).astype(BF16)
        zeros[...] = jnp.zeros_like(zeros)
        for q in range(SLOTS):

            @pl.when(has_ref[q] == 0)
            def _(q=q):
                pltpu.make_async_copy(zeros, out_ref.at[q], sem).start()

    for i in range(group):
        p = step * group + i
        wide = jnp.concatenate([fine_ref[i, f] for f in range(fields)], axis=1)
        mean = jnp.dot(averaging[...], wide, preferred_element_type=F32).astype(BF16)
        for f in range(fields):
            results[p, f] = mean[:, f * LANES : (f + 1) * LANES]
        pltpu.make_async_copy(results.at[p], out_ref.at[slot_ref[p]], sem).start()

    @pl.when(step == steps - 1)
    def _():
        plain = pltpu.make_async_copy(results.at[:, pl.ds(EARLY, fields - EARLY)], plain_ref, plain_sem)
        plain.start()
        plain.wait()
        pltpu.make_async_copy(out_ref, out_ref, sem).wait()


def restrict(slot, has_patch, fine_map, fine_cells, after):
    per_owner, fields, fine, _ = fine_cells.shape
    group = 4
    steps = per_owner // group
    return pl.pallas_call(
        lambda *refs: restrict_kernel(steps, group, fields, *refs),
        grid=(steps,),
        out_shape=[
            jax.ShapeDtypeStruct((SLOTS, fields, PB, LANES), BF16),
            jax.ShapeDtypeStruct((per_owner, fields - EARLY, PB, LANES), BF16),
        ],
        in_specs=[
            SMEM,
            SMEM,
            pl.BlockSpec((1, fine), lambda i: (0, 0)),
            pl.BlockSpec((group, fields, fine, LANES), lambda i: (i, 0, 0, 0)),
            ANY,
        ],
        out_specs=[ANY, ANY],
        scratch_shapes=[
            pltpu.VMEM((PB, fine), BF16),
            pltpu.VMEM((fields, PB, LANES), BF16),
            pltpu.VMEM((per_owner, fields, PB, LANES), BF16),
            pltpu.SemaphoreType.DMA,
            pltpu.SemaphoreType.DMA,
        ],
        compiler_params=PARAMS,
        cost_estimate=cost(fields * 2**22, 2 * per_owner * fields * PB * fine * LANES),
    )(slot, has_patch, fine_map.reshape(1, fine), fine_cells, after)


def local_kernel(z_ref, late_ref, first_ref, patches_ref, coarse_ref, *rest):
    *outs, stay_ref, stage, stay, into, away, stay_sem = rest
    own = patches_ref.shape[0] // NZ
    for n, r in enumerate(SEND_ORDER):
        for j in range(QUARTER):
            box = jnp.maximum(late_ref[r * QUARTER + j], 0)
            pltpu.make_async_copy(coarse_ref.at[pl.ds(EARLY, F - EARLY), box], stage.at[n, j], into.at[n]).start()
        share = pl.ds((z_ref[0] + r) % NZ * own, own)
        pltpu.make_async_copy(patches_ref.at[share], stage.at[n, pl.ds(QUARTER, own)], into.at[n]).start()
    for j in range(QUARTER):
        pltpu.make_async_copy(coarse_ref.at[:, first_ref[j]], stay.at[j], stay_sem.at[0]).start()
    for n, r in enumerate(SEND_ORDER):
        pltpu.make_async_copy(outs[r], stage.at[n], into.at[n]).wait()
        for j in range(QUARTER):

            @pl.when(late_ref[r * QUARTER + j] < 0)
            def _(n=n, j=j):
                stage[n, j] = jnp.zeros_like(stage[n, j])

        pltpu.make_async_copy(stage.at[n], outs[r], away.at[n]).start()
    pltpu.make_async_copy(stay_ref, stay, stay_sem.at[0]).wait()
    pltpu.make_async_copy(stay, stay_ref, stay_sem.at[1]).start()
    for n, r in enumerate(SEND_ORDER):
        pltpu.make_async_copy(stage.at[n], outs[r], away.at[n]).wait()
    pltpu.make_async_copy(stay, stay_ref, stay_sem.at[1]).wait()


def local_part(z, late, first, patches, coarse):
    shape = (QUARTER + patches.shape[0] // NZ, patches.shape[1], PB, LANES)
    stay = (QUARTER, F, PB, LANES)
    return pl.pallas_call(
        local_kernel,
        out_shape=[jax.ShapeDtypeStruct(shape, BF16)] * NZ + [jax.ShapeDtypeStruct(stay, BF16)],
        in_specs=[SMEM, SMEM, SMEM, ANY, ANY],
        out_specs=[ANY] * (NZ + 1),
        scratch_shapes=[
            pltpu.VMEM((NZ, *shape), BF16),
            pltpu.VMEM(stay, BF16),
            pltpu.SemaphoreType.DMA((NZ,)),
            pltpu.SemaphoreType.DMA((NZ,)),
            pltpu.SemaphoreType.DMA((2,)),
        ],
        compiler_params=PARAMS,
        cost_estimate=cost(2**22),
    )(z, late, first, patches, coarse)


def merge_kernel(order_ref, pick_ref, received_ref, coarse_ref, after_ref, *rest):
    outs, (stage, into, away) = rest[:-3], rest[-3:]
    fields = pl.ds(0, EARLY)
    for n, r in enumerate(SEND_ORDER):
        for j in range(QUARTER):
            k = r * QUARTER + j
            box = pick_ref[k]

            @pl.when(box < 0)
            def _(n=n, j=j, k=k):
                pltpu.make_async_copy(received_ref.at[order_ref[k], fields], stage.at[n, j], into.at[n, j // LOT]).start()

            @pl.when(box >= 0)
            def _(n=n, j=j, box=box):
                pltpu.make_async_copy(coarse_ref.at[fields, box], stage.at[n, j], into.at[n, j // LOT]).start()

    stage_out(stage, [outs[r] for r in SEND_ORDER], into, away)


def merge(order, pick, received, coarse, after):
    shape = (QUARTER, EARLY, PB, LANES)
    return pl.pallas_call(
        merge_kernel,
        out_shape=[jax.ShapeDtypeStruct(shape, BF16)] * NZ,
        in_specs=[SMEM, SMEM, ANY, ANY, ANY],
        out_specs=[ANY] * NZ,
        scratch_shapes=[pltpu.VMEM((NZ, *shape), BF16)] + [pltpu.SemaphoreType.DMA((NZ, QUARTER // LOT)), pltpu.SemaphoreType.DMA((NZ,))],
        compiler_params=PARAMS,
        cost_estimate=cost(4 * 2**20),
    )(order, pick, received, coarse, after)


def output_kernel(slots_ref, out_ref, stage, into, away):
    ins = [pltpu.make_async_copy(slots_ref.at[:, f], stage.at[f], into.at[f]) for f in range(F)]
    outs = [pltpu.make_async_copy(stage.at[f], out_ref.at[f], away.at[f]) for f in range(F)]
    for copy in ins:
        copy.start()
    for copy, out in zip(ins, outs):
        copy.wait()
        out.start()
    for out in outs:
        out.wait()


def slot_output(slots):
    return pl.pallas_call(
        output_kernel,
        out_shape=jax.ShapeDtypeStruct((F, SLOTS, PB, LANES), BF16),
        in_specs=[ANY],
        out_specs=ANY,
        scratch_shapes=[pltpu.VMEM((F, SLOTS, PB, LANES), BF16)] + [pltpu.SemaphoreType.DMA((F,))] * 2,
        compiler_params=SMALL,
        cost_estimate=cost(8 * 2**20),
    )(slots)


def gram_kernel(offset, has_before, scale, weight_ref, place_ref, x0, x1, x2, x3, *rest):
    f = pl.program_id(0)
    before_ref, total = rest[0], rest[-1]

    @pl.when(f == 0)
    def _():
        total[...] = before_ref[...] if has_before else jnp.zeros_like(total)

    cells = x0.shape[0] * PB
    wide = jnp.concatenate([x[...].reshape(cells, LANES) for x in (x0, x1, x2, x3)], axis=1)
    product = lax.dot_general(wide, wide, (((0,), (0,)), ((), ())), preferred_element_type=F32)
    for b in range(NZ):
        total[b] += weight_ref[offset + f] * product[:, b * LANES : (b + 1) * LANES]

    if scale is not None:

        @pl.when(f == pl.num_programs(0) - 1)
        def _():
            for level in range(2):

                @pl.when(place_ref[1] == level)
                def _(level=level):
                    split_pieces(place_ref[0], total, scale, rest[-3], rest[-2], level)


def split_pieces(z, total, scale, keep_ref, send_ref, level):
    rows = 4
    per_group = LANES // (2 * rows)
    for a in range(NZ):
        ga = (GRAM_ORDER[a] + z) % NZ
        for b in range(NZ):
            gb = (GRAM_ORDER[b] + z) % NZ
            for half in range(2):
                out_ref = keep_ref if half == level else send_ref
                for i in range(rows):
                    part = total[b, pl.ds(a * LANES + half * rows + i, per_group, stride=2 * rows), :]
                    start = ga * per_group * NZ * rows + gb * rows + i
                    out_ref[pl.ds(start, per_group, stride=NZ * rows), :] = part * scale


def gram(weight, place, xs, before=None, offset=0, scale=None, effort=1, after=None):
    boxes, fields = xs[0].shape[:2]
    block = pl.BlockSpec((boxes, 1, PB, LANES), lambda f: (0, f, 0, 0))
    whole = pl.BlockSpec((NZ, S, LANES), lambda f: (0, 0, 0))
    more = [] if before is None else [(before, whole)]
    if after is not None:
        more.append((after, ANY))
    last = scale is not None
    return pl.pallas_call(
        lambda *refs: gram_kernel(offset, before is not None, scale, *refs),
        grid=(fields,),
        out_shape=[jax.ShapeDtypeStruct((S * NZ // 2, LANES), F32)] * 2 if last else jax.ShapeDtypeStruct((NZ, S, LANES), F32),
        in_specs=[SMEM, SMEM] + [block] * NZ + [spec for _, spec in more],
        out_specs=[pl.BlockSpec((S * NZ // 2, LANES), lambda f: (0, 0))] * 2 if last else whole,
        scratch_shapes=[pltpu.VMEM((NZ, S, LANES), F32)] if last else [],
        compiler_params=SMALL,
        cost_estimate=cost(effort * (fields * 2**20 + 2**21), effort * 2 * fields * boxes * PB * S * S),
    )(weight, place, *xs, *[x for x, _ in more])


def shift(x, by):
    return lax.ppermute(x, "snap", [(i, (i + by) % NZ) for i in range(NZ)])


def exchange(sends):
    return tuple(shift(sends[(NZ - g) % NZ], (NZ - g) % NZ) if g else sends[0] for g in GRAM_ORDER)


def anchor(*behind):
    def kernel(*refs):
        refs[-1][...] = jnp.zeros_like(refs[-1])

    return pl.pallas_call(
        kernel,
        out_shape=jax.ShapeDtypeStruct((8, LANES), F32),
        in_specs=[ANY] * len(behind),
        out_specs=VMEM,
        compiler_params=PARAMS,
        cost_estimate=cost(2**30, 2**40),
    )(*behind)


def on_device(coarse, fine_cells, patch_block, fine_map, field_weight):
    own = lax.axis_index(XY).astype(I32)
    z = lax.axis_index("snap").astype(I32)
    per_owner = fine_cells.shape[0]
    blocks_dev = coarse.shape[1] // PB
    coarse_boxes = coarse.reshape(F, blocks_dev, PB, LANES)
    order, place, first = free_boxes(patch_block, own, z, blocks_dev)
    at_z = z.reshape(1)
    spot = jnp.stack([z, lax.axis_index("level").astype(I32)])

    (across,) = gather_free(first, coarse_boxes, (2,), field_weight)
    patch_block, across = lax.optimization_barrier((patch_block, across))
    slot, has_patch, pick, late = tables(patch_block, own, order, place, per_owner, blocks_dev)
    outgoing, patches = restrict(slot, has_patch, fine_map, fine_cells, across)
    up, down = gather_free(first, coarse_boxes, (1, 3), patches)
    received = lax.all_to_all(outgoing, XY, split_axis=0, concat_axis=0, tiled=True)
    *local_sends, stay = local_part(at_z, late, first, patches, coarse_boxes)
    free = exchange((stay, up, across, down))
    local = exchange(local_sends)

    slots = exchange(merge(order, pick, received, coarse_boxes, anchor(free[1], local_sends[0])))
    total = gram(field_weight, spot, free, effort=400)
    total = gram(field_weight, spot, local, total, EARLY, effort=400)

    scale = 1.0 / (F * coarse.shape[1] * OWNERS)
    keep, send = gram(field_weight, spot, slots, total, 0, scale)

    shares = keep + lax.ppermute(send, "level", [(0, 1), (1, 0)])
    collected = lax.all_to_all(shares, ("snap", "tile"), split_axis=0, concat_axis=0, tiled=True)
    restricted = slot_output(received)
    summed = jnp.sum(collected.reshape(S // 8, NZ, NZ, LANES), axis=0)
    gram_matrix = summed.transpose(1, 0, 2).reshape(S // 128, S)
    return (gram_matrix, restricted)


def solution(mesh):
    return jax.shard_map(
        on_device,
        mesh=mesh,
        in_specs=(
            P(None, ("tile", "level"), "snap"),
            P(("tile", "level"), None, None, "snap"),
            P(),
            P(),
            P(),
        ),
        out_specs=(P(("snap", "tile", "level"), None), P(None, ("tile", "level"), None, "snap")),
        check_vma=False,
    )
```
